32 devices in a mesh: groups: 2 (over x), tensor: 16 (over z, y, core).
Axes of the slice: x: 2, y: 2, z: 4, core: 2. Of those that a mesh axis runs over, the one named last changes fastest.
Arguments:
- hidden: bfloat16 [384, 16384], P('groups', 'tensor'), parts along dimension 0, may hold values from -6 to 6
- w_query: bfloat16 [16384, 8192], P(None, 'tensor'), may hold values from -0.046875 to 0.046875
- w_out: bfloat16 [8192, 16384], P('tensor'), may hold values from -0.09375 to 0.09375
- new_kv: bfloat16 [384, 2, 4, 128], P(('groups', 'tensor')), parts along dimension 0, may hold values from -6 to 6
- prefix_kv: bfloat16 [32, 3, 2, 4, 512, 128], P(('groups', 'tensor')), parts along dimension 0, may hold values from -700 to 700
- suffix_kv: bfloat16 [384, 2, 4, 256, 128], P(('groups', 'tensor')), parts along dimension 0, may hold values from -6 to 6
- parents: int32 [384], P(('groups', 'tensor')), parts along dimension 0, may hold values from 0 to 7
- lengths: int32 [384], P(('groups', 'tensor')), parts along dimension 0, may hold values from 1 to 256, 36864 in all
Outputs:
- attended: bfloat16 [384, 16384], P('groups', 'tensor'), parts along dimension 0
The draws below stay inside these ranges and needn't reach their ends.
There are 2 independent parts, one for each index of `groups`. The reference program is written for one: setup_inputs(seed, part) draws one part's arguments, and reference() takes and returns one part's arrays. A program takes and returns all parts, laid end to end along the dimension named above; an argument that names none is the same for every part. Nothing has to cross between parts.
Inputs may be any that keep to these rules, and one draw needn't show every extreme that they name: `lengths`: some page is full.
All inputs are finite; a program needn't handle non-finite values. No bound on the sum of `lengths` on one device may be relied on, other than what follows from the above.
Results may differ from the reference program's by a relative error of at most 0.02.
The reference program's roundings to bfloat16 on the way count: a program that leaves them out, or rounds other values in their place, can miss the bound.
Values may be sent and summed in bfloat16 or wider, within the bound.
No kernel may reach another device: no remote copies, remote signals or barrier semaphores. Data moves between devices by JAX's collectives and lax.ppermute only.
A program may use at most 192 MiB of HBM per device.

```python
import math
import jax
import jax.numpy as jnp
import numpy as np
from jax import lax

D = 16384
HEADS = 64
KV = 4
HD = 128
BEAMS = 8
PROMPTS_DEV = 3
PREFIX = 1024
SUFFIX = 256
ROWS = 192
PROMPTS = 24
N_TENSOR = 16


def draw_prefix_kv(key, part):
    key = jax.random.fold_in(key, 11)
    key_base = jax.random.fold_in(key, 0)
    dims_all = (N_TENSOR, PROMPTS_DEV, 2, KV, PREFIX // 2, HD)
    return jnp.clip(jax.random.normal(key_base, dims_all, jnp.float32), -6.0, 6.0).astype(jnp.bfloat16)


def plant(result, own_key, least, largest):
    longest = result.shape.index(max(result.shape))
    spots = []
    for shift in (0, 1):
        where = [jax.random.randint(jax.random.fold_in(own_key, axis), (), 0, length) for axis, length in enumerate(result.shape)]
        where[longest] = (where[longest] + shift) % result.shape[longest]
        spots.append(tuple(where))
    return result.at[spots[0]].set(least).at[spots[1]].set(largest)


def raised(array, rng, source, target, parts, factor):
    def block_of(axis_at):
        return (jnp.arange(array.shape[axis_at]) // (array.shape[axis_at] // parts)).reshape((-1,) + (1,) * (array.ndim - 1 - axis_at))

    near = jax.random.permutation(rng, parts)[block_of(target)]
    other_side = (block_of(target) + parts // 2) % parts
    return jnp.where((block_of(source) == near) | (block_of(source) == other_side), factor * array, array)


def block_levels(stream_key, dims, shards, smallest, largest):
    factor_of, own = 1.0, jax.random.fold_in(stream_key, 6)
    for dim, parts in shards:
        draws = jnp.exp(jax.random.uniform(jax.random.fold_in(own, dim), (parts,), jnp.float32, smallest / len(shards), largest / len(shards)))
        factor_of = factor_of * jnp.repeat(draws, dims[dim] // parts).reshape([-1 if axis == dim else 1 for axis in range(len(dims))])
    return factor_of


def split_up(amount, total, reach, lean):
    weights = [(1 << 20) // math.isqrt(standing ** lean) + 1 for standing in range(2, amount + 1)]
    spare, counts = total - reach - (amount - 1), [1] * (amount - 1)
    while spare > 0:
        candidates = [i for i in range(amount - 1) if counts[i] < reach]
        pool, remaining = sum([weights[i] for i in candidates]), spare
        for i in candidates:
            addition = min(reach - counts[i], max(1, remaining * weights[i] // pool), spare)
            counts[i] = counts[i] + addition
            spare = spare - addition
    return np.array([reach] + counts)


def ragged_sizes(own_key, amount, total, bound, slope):
    if amount == 2:
        one = jax.random.randint(own_key, (), max(1, total - bound), min(bound, total - 1) + 1)
        return jnp.stack([one, total - one])
    sizes = jnp.asarray(split_up(amount, total, bound, slope), jnp.int32)
    pairs = (amount - 1) // 2
    source_of, taker = sizes[1:1 + 2 * pairs:2], sizes[2:2 + 2 * pairs:2]
    margin = jnp.minimum(source_of - 1, bound - taker)
    moved = jax.random.randint(jax.random.fold_in(own_key, 1), (pairs,), 0, 1 << 20) % (margin + 1)
    sizes = sizes.at[1:1 + 2 * pairs:2].set(source_of - moved).at[2:2 + 2 * pairs:2].set(taker + moved)
    return sizes[jax.random.permutation(jax.random.fold_in(own_key, 2), amount)]


def gaussian(stream_key, dims, scale, reach, cuts=(), kind=jnp.bfloat16):
    gain = block_levels(stream_key, dims, cuts, -0.22, 0.18) if cuts else 1.0
    drawn = jax.random.normal(stream_key, dims, jnp.float32) * scale * gain
    return jnp.minimum(jnp.maximum(drawn, -reach), reach).astype(kind)


def noise_with(key, extent, spread, bound, cuts, heavy, kind=jnp.bfloat16):
    drawn = spread * jax.random.normal(key, extent, jnp.float32)
    if cuts:
        drawn = drawn * block_levels(key, extent, cuts, -0.22, 0.18)
    return jnp.clip(raised(drawn, jax.random.fold_in(key, 3), *heavy), -bound, bound).astype(kind)


def setup_inputs(seed: int = 0, part: int = 0) -> dict:
    key_list = jax.random.split(jax.random.key(seed), 9)
    part_keys = jax.random.split(jax.random.fold_in(key_list[8], part), 9)
    return {
        "hidden": gaussian(part_keys[0], (ROWS, D), 1.0, 6.0, ((1, 16),)),
        "w_query": gaussian(key_list[1], (D, HEADS * HD), D ** -0.5, 0.046875, ((1, 16),)),
        "w_out": noise_with(key_list[2], (HEADS * HD, D), (HEADS * HD) ** -0.5, 0.09375, ((0, 16),), (0, 1, 16, 2.0)),
        "new_kv": gaussian(part_keys[3], (ROWS, 2, KV, HD), 1.0, 6.0, ((0, 16),)),
        "prefix_kv": draw_prefix_kv(jax.random.fold_in(jax.random.fold_in(key_list[8], part), 71), part),
        "suffix_kv": gaussian(part_keys[5], (ROWS, 2, KV, SUFFIX, HD), 1.0, 6.0, ((0, 16),)),
        "parents": plant(jax.random.randint(part_keys[6], (ROWS,), 0, BEAMS), jax.random.fold_in(part_keys[6], 1), 0, BEAMS - 1).astype(jnp.int32),
        "lengths": ragged_sizes(part_keys[7], ROWS, ROWS * SUFFIX * 3 // 4, SUFFIX, 2).astype(jnp.int32),
    }


big_negative = -1e30
rope_base = 500000.0


def rotate(queries, position):
    half_size = HD // 2
    frequency = rope_base ** (-jnp.arange(half_size, dtype=jnp.float32) * 2.0 / HD)
    angles = position.astype(jnp.float32)[..., None, None] * frequency
    cosine = jnp.cos(angles)
    sines = jnp.sin(angles)
    entries = queries.astype(jnp.float32)
    lower_half = entries[..., :half_size]
    upper_half = entries[..., half_size:]
    turned = jnp.concatenate([lower_half * cosine - upper_half * sines, upper_half * cosine + lower_half * sines], axis=-1)
    return (turned * (HD ** -0.5)).astype(jnp.bfloat16)


def to_prompts(rows_all):
    trailing = rows_all.shape[1:]
    arranged = rows_all.reshape((N_TENSOR // 2, 2, PROMPTS_DEV, BEAMS // 2) + trailing)
    arranged = jnp.swapaxes(arranged, 1, 2)
    return arranged.reshape((PROMPTS, BEAMS) + trailing)


def from_prompts(per_prompt):
    trailing = per_prompt.shape[2:]
    arranged = per_prompt.reshape((N_TENSOR // 2, PROMPTS_DEV, 2, BEAMS // 2) + trailing)
    arranged = jnp.swapaxes(arranged, 1, 2)
    return arranged.reshape((ROWS,) + trailing)


def reference(hidden, w_query, w_out, new_kv, prefix_kv, suffix_kv, parents, lengths):
    per_kv = HEADS // KV
    width = HEADS * HD // N_TENSOR
    query = jnp.dot(hidden, w_query, preferred_element_type=jnp.float32).astype(jnp.bfloat16)
    queries = to_prompts(query.reshape(ROWS, HEADS, HD))
    parent_p = to_prompts(parents)
    length_p = to_prompts(lengths)
    new_p = to_prompts(new_kv)
    pages_p = to_prompts(suffix_kv)
    prefix = prefix_kv.reshape(N_TENSOR // 2, 2, PROMPTS_DEV, 2, KV, PREFIX // 2, HD)
    prefix = jnp.transpose(prefix, (0, 2, 3, 4, 1, 5, 6)).reshape(PROMPTS, 2, KV, PREFIX, HD)

    def attend_one(per_prompt):
        query_p, parent_one, length_one, new_one, pages_one, prefix_one = per_prompt
        page_len = jnp.take(length_one, parent_one)
        chosen = jnp.take(pages_one, parent_one, axis=0)
        grouped = rotate(query_p, PREFIX + page_len).astype(jnp.float32).reshape(BEAMS, KV, per_kv, HD)
        prefix_keys = prefix_one[0].astype(jnp.float32)
        prefix_values = prefix_one[1].astype(jnp.float32)
        page_keys = chosen[:, 0].astype(jnp.float32)
        page_values = chosen[:, 1].astype(jnp.float32)
        scores_pre = jnp.einsum("bkge,kne->bkgn", grouped, prefix_keys)
        scores_suf = jnp.einsum("bkge,bkse->bkgs", grouped, page_keys)
        scores_new = jnp.einsum("bkge,bke->bkg", grouped, new_one[:, 0].astype(jnp.float32))
        usable = (jnp.arange(SUFFIX)[None, :] < page_len[:, None])[:, None, None, :]
        highest = jnp.maximum(jnp.max(scores_pre, axis=-1), jnp.max(jnp.where(usable, scores_suf, big_negative), axis=-1))
        highest = jnp.maximum(highest, scores_new)
        weights_pre = jnp.exp(scores_pre - highest[..., None])
        weights_suf = jnp.where(usable, jnp.exp(scores_suf - highest[..., None]), 0.0)
        weights_new = jnp.exp(scores_new - highest)
        weight_sum = jnp.sum(weights_pre, axis=-1) + jnp.sum(weights_suf, axis=-1) + weights_new
        weighted = jnp.einsum("bkgn,kne->bkge", weights_pre.astype(jnp.bfloat16).astype(jnp.float32), prefix_values)
        weighted = weighted + jnp.einsum("bkgs,bkse->bkge", weights_suf.astype(jnp.bfloat16).astype(jnp.float32), page_values)
        weighted = weighted + weights_new.astype(jnp.bfloat16).astype(jnp.float32)[..., None] * new_one[:, 1].astype(jnp.float32)[:, :, None, :]
        return (weighted / weight_sum[..., None]).astype(jnp.bfloat16).reshape(BEAMS, HEADS * HD)

    heads_out = lax.map(attend_one, (queries, parent_p, length_p, new_p, pages_p, prefix))
    heads_out = from_prompts(heads_out)
    blocks = jnp.swapaxes(heads_out.reshape(ROWS, N_TENSOR, width), 0, 1)
    weight_blocks = w_out.reshape(N_TENSOR, width, D)

    def add_partial(running, operands):
        partial_value = jnp.dot(operands[0], operands[1], preferred_element_type=jnp.float32).astype(jnp.bfloat16)
        return running + partial_value.astype(jnp.float32), None

    running, _ = lax.scan(add_partial, jnp.zeros((ROWS, D), jnp.float32), (blocks, weight_blocks))
    return running.astype(jnp.bfloat16)
```

```python
import functools

import jax
import jax.numpy as jnp
from jax import lax
from jax.experimental import pallas as pl
from jax.experimental.pallas import tpu as pltpu
from jax.sharding import PartitionSpec as P

HEADS = 64
KV = 4
HD = 128
BEAMS = 8
HALF = BEAMS // 2

rope_base = 500000.0
big_negative = -1e30
f32 = jnp.float32
bf16 = jnp.bfloat16
MIB = 1024 * 1024
VMEM_LIMIT = 48 * MIB


def ring_chips(count):
    if count == 8:
        return [0, 2, 4, 6, 7, 5, 3, 1]
    return list(range(count))


def send(block, route):
    return lax.ppermute(block, "tensor", route)


def tied(*values):
    return lax.optimization_barrier(values)


def along(order, step):
    count = len(order)
    return [
        (2 * order[i] + c, 2 * order[(i + step) % count] + c)
        for i in range(count)
        for c in range(2)
    ]


def make_plan(order, hops):
    chips = len(order)
    arrive = [0] + [d for s in range(1, hops) for d in (-s, s)] + [hops]
    leave = [hops] + [d for s in range(hops - 1, 0, -1) for d in (s, -s)] + [0]
    rows = []
    for t in range(2 * chips):
        at = order.index(t // 2)
        rows.append([order[(at + d) % chips] for d in arrive + leave] + [t % 2])
    return jnp.asarray(rows, jnp.int32)


def split_kernel(chips, by_rows, plan_ref, whole, part, buf, in_sems, out_sems):
    other = 1 - plan_ref[2 * chips]
    size = (part.shape[0] if by_rows else part.shape[1]) // chips
    ins, outs = [], []
    for i in range(chips):
        start = pl.multiple_of((2 * i + other) * size, size)
        if by_rows:
            source, target = whole.at[pl.ds(start, size)], part.at[pl.ds(i * size, size)]
        else:
            source, target = whole.at[:, pl.ds(start, size)], part.at[:, pl.ds(i * size, size)]
        ins.append(pltpu.make_async_copy(source, buf.at[i], in_sems.at[i]))
        outs.append(pltpu.make_async_copy(buf.at[i], target, out_sems.at[i]))
    for copy in ins:
        copy.start()
    for before, after in zip(ins, outs):
        before.wait()
        after.start()
    for copy in outs:
        copy.wait()


def others_half(whole, plan, chips, by_rows):
    shape = (whole.shape[0] // 2, whole.shape[1]) if by_rows else (whole.shape[0], whole.shape[1] // 2)
    block = (shape[0] // chips, shape[1]) if by_rows else (shape[0], shape[1] // chips)
    anywhere = pl.BlockSpec(memory_space=pl.ANY)
    return pl.pallas_call(
        functools.partial(split_kernel, chips, by_rows),
        in_specs=[pl.BlockSpec(memory_space=pltpu.SMEM), anywhere],
        out_specs=anywhere,
        out_shape=jax.ShapeDtypeStruct(shape, whole.dtype),
        scratch_shapes=[
            pltpu.VMEM((chips,) + block, whole.dtype),
            pltpu.SemaphoreType.DMA((chips,)),
            pltpu.SemaphoreType.DMA((chips,)),
        ],
        cost_estimate=pl.CostEstimate(flops=0, bytes_accessed=2 * whole.size, transcendentals=0),
        compiler_params=pltpu.CompilerParams(vmem_limit_bytes=VMEM_LIMIT),
    )(plan, whole)


def query_kernel(bases, first, far, with_total, plan_ref, *refs):
    sides = len(far)
    count = sum(len(group) for group in bases)
    blocks = refs[:count]
    weights = refs[count : count + sides]
    before = refs[count + sides : count + 2 * sides] if with_total else None
    totals, buf, sems = refs[-sides - 2 : -2], refs[-2], refs[-1]
    depth = buf.shape[1]
    core = plan_ref[plan_ref.shape[0] - 1]
    copies = []
    for i in range(len(bases)):
        for side in range(sides):
            block = plan_ref[first + i]
            block = block if far[side] else 2 * block + core
            rows = pl.ds(pl.multiple_of(block * depth, depth), depth)
            n = i * sides + side
            copies.append(pltpu.make_async_copy(weights[side].at[rows], buf.at[n], sems.at[n]))
    for copy in copies:
        copy.start()
    for side in range(sides):
        if with_total:
            totals[side][...] = before[side][...]
        else:
            totals[side][...] = jnp.zeros_like(totals[side])
    at = 0
    for i, group in enumerate(bases):
        for side in range(sides):
            n = i * sides + side
            copies[n].wait()
            for g, base in enumerate(group):
                rows = pl.ds(base, blocks[at + g].shape[0])
                totals[side][rows, :] += jnp.dot(
                    blocks[at + g][...], buf[n], preferred_element_type=f32
                )
        at += len(group)


def query_terms(totals, groups, w_own, w_far, plan, first):
    blocks = [block for group in groups for block, _ in group]
    bases = [[base for _, base in group] for group in groups]
    depth = blocks[0].shape[1]
    rows = max(base + block.shape[0] for group in groups for block, base in group)
    weights = [w for w in (w_own, w_far) if w is not None]
    far = [w is w_far for w in weights]
    width = weights[0].shape[1]
    sides = len(weights)
    totals = list(totals) if totals is not None else []
    vmem = pl.BlockSpec(memory_space=pltpu.VMEM)
    return pl.pallas_call(
        functools.partial(query_kernel, bases, first, far, bool(totals)),
        in_specs=[pl.BlockSpec(memory_space=pltpu.SMEM)]
        + [vmem] * len(blocks)
        + [pl.BlockSpec(memory_space=pl.ANY)] * sides
        + [vmem] * len(totals),
        out_specs=[vmem] * sides,
        out_shape=[jax.ShapeDtypeStruct((rows, width), f32)] * sides,
        scratch_shapes=[
            pltpu.VMEM((sides * len(groups), depth, width), bf16),
            pltpu.SemaphoreType.DMA((sides * len(groups),)),
        ],
        cost_estimate=pl.CostEstimate(
            flops=2 * sides * sum(block.size for block in blocks) * width,
            bytes_accessed=2 * sides * len(groups) * depth * width
            + 2 * sum(block.size for block in blocks),
            transcendentals=0,
        ),
        compiler_params=pltpu.CompilerParams(vmem_limit_bytes=VMEM_LIMIT),
    )(plan, *blocks, *weights, *totals)


def out_kernel(first, amount, parts, plan_ref, own, far, w_own, w_far, *refs):
    outs, buf, sems = refs[:-2], refs[-2], refs[-1]
    width = buf.shape[2]
    core = plan_ref[plan_ref.shape[0] - 1]
    copies = []
    for i in range(amount):
        block = plan_ref[first + i]
        for side, weights in enumerate((w_own, w_far)):
            column = block if side else 2 * block + core
            columns = pl.ds(pl.multiple_of(column * width, width), width)
            n = 2 * i + side
            copies.append(pltpu.make_async_copy(weights.at[:, columns], buf.at[n], sems.at[n]))
    for copy in copies:
        copy.start()
    for i in range(amount):
        copies[2 * i].wait()
        value = jnp.dot(own[...], buf[2 * i], preferred_element_type=f32)
        copies[2 * i + 1].wait()
        value = value + jnp.dot(far[...], buf[2 * i + 1], preferred_element_type=f32)
        rows = value.shape[0] // parts
        for p in range(parts):
            target = outs[i * parts + p]
            target[...] = value[p * rows : (p + 1) * rows].astype(target.dtype)


def out_terms(own, far, w_own, w_far, plan, first, amount, width, kind, parts=1):
    rows, depth = own.shape
    vmem = pl.BlockSpec(memory_space=pltpu.VMEM)
    anywhere = pl.BlockSpec(memory_space=pl.ANY)
    return pl.pallas_call(
        functools.partial(out_kernel, first, amount, parts),
        in_specs=[pl.BlockSpec(memory_space=pltpu.SMEM), vmem, vmem, anywhere, anywhere],
        out_specs=[vmem] * (amount * parts),
        out_shape=[jax.ShapeDtypeStruct((rows // parts, width), kind)] * (amount * parts),
        scratch_shapes=[
            pltpu.VMEM((2 * amount, depth, width), bf16),
            pltpu.SemaphoreType.DMA((2 * amount,)),
        ],
        cost_estimate=pl.CostEstimate(
            flops=4 * rows * depth * width * amount,
            bytes_accessed=4 * depth * width * amount + 4 * rows * width * amount,
            transcendentals=0,
        ),
        compiler_params=pltpu.CompilerParams(vmem_limit_bytes=VMEM_LIMIT),
    )(plan, own, far, w_own, w_far)


def attend_kernel(
    source_ref, row_ref, length_ref,
    q_ref, cos_ref, sin_ref, new_ref, prefix_own, prefix_far, suffix_own, suffix_far,
    out_ref, prefix_buf, page_buf, q_buf, o_buf, prefix_sem, page_sem,
):
    prompts = prefix_buf.shape[0]
    devices, rows, width = q_ref.shape
    heads_here = width // HD
    per_kv = devices // KV
    page = page_buf.shape[3]
    group_rows = per_kv * heads_here * HALF

    def prefix_copies(j):
        return [
            pltpu.make_async_copy(prefix_own.at[0, j], prefix_buf.at[j, 0], prefix_sem.at[j, 0]),
            pltpu.make_async_copy(prefix_far.at[0, j], prefix_buf.at[j, 1], prefix_sem.at[j, 1]),
        ]

    def fetch(j):
        for copy in prefix_copies(j):
            copy.start()
        for b in range(HALF):
            r = j * HALF + b

            @pl.when(source_ref[r] == 0)
            def _():
                pltpu.make_async_copy(
                    suffix_own.at[row_ref[r]], page_buf.at[r], page_sem.at[r]
                ).start()

            @pl.when(source_ref[r] != 0)
            def _():
                pltpu.make_async_copy(
                    suffix_far.at[row_ref[r]], page_buf.at[r], page_sem.at[r]
                ).start()

    fetch(0)
    q_buf[...] = q_ref[...].astype(f32)
    row_beam = lax.broadcasted_iota(jnp.int32, (group_rows, page), 0) % HALF
    position = lax.broadcasted_iota(jnp.int32, (group_rows, page), 1)
    nt = (((1,), (1,)), ((), ()))

    def spread(four):
        return jnp.concatenate([four] * (group_rows // HALF), axis=0)

    for j in range(prompts):
        beams = slice(j * HALF, (j + 1) * HALF)
        cosine = spread(cos_ref[beams, :])
        sines = spread(sin_ref[beams, :])
        for copy in prefix_copies(j):
            copy.wait()
        masks = []
        for b in range(HALF):
            r = j * HALF + b
            pltpu.make_async_copy(suffix_own.at[0], page_buf.at[r], page_sem.at[r]).wait()
            masks.append((row_beam == b) & (position < length_ref[r]))
        if j + 1 < prompts:
            fetch(j + 1)
        for k in range(KV):
            pieces = [
                q_buf[k * per_kv + t, beams, h * HD : (h + 1) * HD]
                for t in range(per_kv)
                for h in range(heads_here)
            ]
            query = jnp.concatenate(pieces, axis=0)
            turned = query * cosine + pltpu.roll(query, HD // 2, 1) * sines
            turned = (turned * HD ** (-0.5)).astype(bf16)
            keys = [prefix_buf[j, 0, 0, k], prefix_buf[j, 1, 0, k]]
            values = [prefix_buf[j, 0, 1, k], prefix_buf[j, 1, 1, k]]
            scores = [lax.dot_general(turned, key, nt, preferred_element_type=f32) for key in keys]
            for b in range(HALF):
                r = j * HALF + b
                raw = lax.dot_general(turned, page_buf[r, 0, k], nt, preferred_element_type=f32)
                scores.append(jnp.where(masks[b], raw, big_negative))
                values.append(page_buf[r, 1, k])
            new_key = spread(new_ref[beams, k * HD : (k + 1) * HD])
            new_value = spread(new_ref[beams, (KV + k) * HD : (KV + k + 1) * HD])
            new_score = jnp.sum(turned.astype(f32) * new_key, axis=1, keepdims=True)
            highest = new_score
            for score in scores:
                highest = jnp.maximum(highest, jnp.max(score, axis=1, keepdims=True))
            new_weight = jnp.exp(new_score - highest)
            weight_sum = new_weight
            weighted = new_weight.astype(bf16).astype(f32) * new_value
            for score, value in zip(scores, values):
                weight = jnp.exp(score - highest)
                weight_sum = weight_sum + jnp.sum(weight, axis=1, keepdims=True)
                weighted = weighted + jnp.dot(
                    weight.astype(bf16), value, preferred_element_type=f32
                )
            result = weighted / weight_sum
            for t in range(per_kv):
                for h in range(heads_here):
                    at = (t * heads_here + h) * HALF
                    o_buf[k * per_kv + t, beams, h * HD : (h + 1) * HD] = result[at : at + HALF]
    out_ref[...] = o_buf[...].astype(bf16)


def attend(queries, cosine, sines, new_rows, prefix_own, prefix_far, suffix_own, suffix_far,
           source, row, page_len):
    devices, rows, width = queries.shape
    prompts = rows // HALF
    part = prefix_own.shape[4]
    page = suffix_own.shape[3]
    vmem = pl.BlockSpec(memory_space=pltpu.VMEM)
    smem = pl.BlockSpec(memory_space=pltpu.SMEM)
    anywhere = pl.BlockSpec(memory_space=pl.ANY)
    keys = rows * (2 * part + page)
    return pl.pallas_call(
        attend_kernel,
        in_specs=[smem] * 3 + [vmem] * 4 + [anywhere] * 4,
        out_specs=vmem,
        out_shape=jax.ShapeDtypeStruct(queries.shape, bf16),
        scratch_shapes=[
            pltpu.VMEM((prompts, 2) + prefix_own.shape[2:], bf16),
            pltpu.VMEM(suffix_own.shape, bf16),
            pltpu.VMEM(queries.shape, f32),
            pltpu.VMEM(queries.shape, f32),
            pltpu.SemaphoreType.DMA((prompts, 2)),
            pltpu.SemaphoreType.DMA((rows,)),
        ],
        cost_estimate=pl.CostEstimate(
            flops=4 * keys * HEADS * HD,
            bytes_accessed=2 * prefix_own.size * 2 + 2 * suffix_own.size,
            transcendentals=keys * HEADS,
        ),
        compiler_params=pltpu.CompilerParams(vmem_limit_bytes=VMEM_LIMIT),
    )(source, row, page_len, queries, cosine, sines, new_rows,
      prefix_own, prefix_far, suffix_own, suffix_far)


def body(hidden, w_query, w_out, new_kv, prefix_kv, suffix_kv, parents, lengths):
    count = lax.axis_size("tensor")
    order = ring_chips(count // 2)
    chips = len(order)
    hops = chips // 2
    me = lax.axis_index("tensor")
    core = me % 2
    plan = lax.dynamic_index_in_dim(make_plan(order, hops), me, keepdims=False)

    onward, backward = along(order, 1), along(order, -1)
    to_core = [(t, t ^ 1) for t in range(count)]
    rows_all, depth = hidden.shape
    rows_here = new_kv.shape[0]
    prompts_here = rows_here // HALF
    prefix_len = 2 * prefix_kv.shape[4]

    def tables(far_len):
        own_len = lengths.reshape(prompts_here, HALF)
        far_len = far_len.reshape(prompts_here, HALF)
        parent = parents.reshape(prompts_here, HALF)
        slot = parent % HALF
        from_far = (parent // HALF) != core
        chosen = [
            jnp.sum(jnp.where(slot[..., None] == jnp.arange(HALF), table[:, None, :], 0), axis=-1)
            for table in (own_len, far_len)
        ]
        page_len = jnp.where(from_far, chosen[1], chosen[0]).reshape(rows_here)
        page_row = (jnp.arange(prompts_here, dtype=jnp.int32)[:, None] * HALF + slot).reshape(rows_here)
        source = from_far.astype(jnp.int32).reshape(rows_here)
        frequency = rope_base ** (-jnp.arange(HD // 2, dtype=f32) * 2.0 / HD)
        angles = (prefix_len + page_len).astype(f32)[:, None] * frequency
        cosine = jnp.cos(angles)
        sines = jnp.sin(angles)
        cosine = jnp.concatenate([cosine, cosine], axis=1)
        sines = jnp.concatenate([-sines, sines], axis=1)
        new_rows = new_kv.astype(f32).reshape(rows_here, 2 * KV * HD)
        return cosine, sines, new_rows, source, page_row, page_len

    cut = rows_all // 2
    a = b = hidden
    blocks = [[(hidden, 0)]]
    own_total = far_total = None
    own_done = far_done = 0
    for s in range(1, hops + 1):
        if s == hops:
            a, b = a[:cut], b[cut:]
        a, b = send(a, onward), send(b, backward)
        if s == 1:
            far_len = send(lengths, to_core)
            prefix_far = send(prefix_kv, to_core)
            wq_send = others_half(w_query, plan, chips, True)
            a, b, far_len, prefix_far, wq_send = tied(a, b, far_len, prefix_far, wq_send)
            wq_far = send(wq_send, to_core)
        else:
            beside = []
            fresh = blocks[own_done:]
            if s == 2:
                own_total = query_terms(None, fresh, w_query, None, plan, 0)
                wo_send = others_half(w_out, plan, chips, False)
                beside = [wo_send] + list(tables(far_len))
            elif s == 3:
                own_total = query_terms(own_total, fresh, w_query, None, plan, own_done)
                far_total = list(query_terms(None, blocks, None, wq_far, plan, 0))
                wo_send, suffix_in, far_total[0] = tied(wo_send, suffix_kv, far_total[0])
                wo_far = send(wo_send, to_core)
                suffix_far = send(suffix_in, to_core)
            else:
                own_total, far_total = query_terms(
                    own_total + far_total, fresh, w_query, wq_far, plan, own_done
                )
                own_total, far_total = [own_total], [far_total]
            far_total = far_total or []
            a, b, *beside = tied(a, b, *own_total, *far_total, *beside)
            own_total, beside = beside[:1], beside[1:]
            if s > 2:
                far_total, beside = beside[:1], beside[1:]
            if s == 2:
                wo_send, cosine, sines, new_rows, source, page_row, page_len = beside
            own_done = len(blocks)
        if s < hops:
            blocks += [[(a, 0)], [(b, 0)]]
        else:
            blocks.append([(a, 0), (b, cut)])
    own_total, far_total = query_terms(
        own_total + far_total, blocks[own_done:], w_query, wq_far, plan, own_done
    )
    query = own_total + send(far_total, to_core)
    query = query.astype(bf16).reshape(count, rows_here, -1)

    query, suffix_far, wo_far = tied(query, suffix_far, wo_far)
    queries = lax.all_to_all(query, "tensor", split_axis=0, concat_axis=0, tiled=True)
    heads = attend(queries, cosine, sines, new_rows, prefix_kv, prefix_far, suffix_kv, suffix_far,
                   source, page_row, page_len)
    heads = lax.all_to_all(heads, "tensor", split_axis=0, concat_axis=0, tiled=True)
    own = heads.reshape(rows_all, -1)
    far = send(own, to_core)

    width = w_out.shape[1] // count

    def out(first, amount, kind, parts=1):
        return out_terms(own, far, w_out, wo_far, plan, chips + first, amount, width, kind, parts)

    up, down = tied(*out(0, 1, bf16, 2))
    a, b = send(up, onward), send(down, backward)
    for s in range(hops - 1, 0, -1):
        up, down = out(1 + 2 * (hops - 1 - s), 2, f32)
        a, b, up, down = tied(a, b, up, down)
        a, b = a.astype(f32), b.astype(f32)
        if s == hops - 1:
            up = jnp.concatenate([up[:cut] + a, up[cut:]], axis=0)
            down = jnp.concatenate([down[:cut], down[cut:] + b], axis=0)
        else:
            up, down = up + a, down + b
        a, b = tied(up.astype(bf16), down.astype(bf16))
        a, b = send(a, onward), send(b, backward)
    [own_term] = out(chips - 1, 1, f32)
    a, b, own_term = tied(a, b, own_term)
    return (own_term + a.astype(f32) + b.astype(f32)).astype(bf16)


def solution(mesh):
    return jax.shard_map(
        body,
        mesh=mesh,
        in_specs=(
            P("groups", "tensor"),
            P(None, "tensor"),
            P("tensor", None),
            P(("groups", "tensor"), None, None, None),
            P(("groups", "tensor"), None, None, None, None, None),
            P(("groups", "tensor"), None, None, None, None),
            P(("groups", "tensor")),
            P(("groups", "tensor")),
        ),
        out_specs=P("groups", "tensor"),
        check_vma=False,
    )
```

```python
import functools

import jax
import jax.numpy as jnp
from jax import lax
from jax.experimental import pallas as pl
from jax.experimental.pallas import tpu as pltpu
from jax.sharding import PartitionSpec as P

HEADS = 64
KV = 4
HD = 128
BEAMS = 8
HALF = BEAMS // 2

rope_base = 500000.0
big_negative = -1e30
f32 = jnp.float32
bf16 = jnp.bfloat16
MIB = 1024 * 1024
VMEM_LIMIT = 48 * MIB
BESIDE = pl.CostEstimate(flops=1000, bytes_accessed=1000, transcendentals=0)


def ring_chips(count):
    if count == 8:
        return [0, 2, 4, 6, 7, 5, 3, 1]
    return list(range(count))


def send(block, route):
    return lax.ppermute(block, "tensor", route)


def tied(*values):
    return lax.optimization_barrier(values)


def along(order, step):
    count = len(order)
    return [
        (2 * order[i] + c, 2 * order[(i + step) % count] + c)
        for i in range(count)
        for c in range(2)
    ]


def make_plan(order, hops):
    chips = len(order)
    arrive = [0] + [d for s in range(1, hops) for d in (-s, s)] + [hops]
    leave = [hops] + [d for s in range(hops - 1, 0, -1) for d in (s, -s)] + [0]
    rows = []
    for t in range(2 * chips):
        at = order.index(t // 2)
        rows.append([order[(at + d) % chips] for d in arrive + leave] + [t % 2])
    return jnp.asarray(rows, jnp.int32)


def split_kernel(chips, by_rows, plan_ref, whole, part, buf, in_sems, out_sems):
    other = 1 - plan_ref[2 * chips]
    size = (part.shape[0] if by_rows else part.shape[1]) // chips
    ins, outs = [], []
    for i in range(chips):
        start = pl.multiple_of((2 * i + other) * size, size)
        if by_rows:
            source, target = whole.at[pl.ds(start, size)], part.at[pl.ds(i * size, size)]
        else:
            source, target = whole.at[:, pl.ds(start, size)], part.at[:, pl.ds(i * size, size)]
        ins.append(pltpu.make_async_copy(source, buf.at[i], in_sems.at[i]))
        outs.append(pltpu.make_async_copy(buf.at[i], target, out_sems.at[i]))
    for copy in ins:
        copy.start()
    for before, after in zip(ins, outs):
        before.wait()
        after.start()
    for copy in outs:
        copy.wait()


def others_half(whole, plan, chips, by_rows):
    shape = (whole.shape[0] // 2, whole.shape[1]) if by_rows else (whole.shape[0], whole.shape[1] // 2)
    block = (shape[0] // chips, shape[1]) if by_rows else (shape[0], shape[1] // chips)
    anywhere = pl.BlockSpec(memory_space=pl.ANY)
    return pl.pallas_call(
        functools.partial(split_kernel, chips, by_rows),
        in_specs=[pl.BlockSpec(memory_space=pltpu.SMEM), anywhere],
        out_specs=anywhere,
        out_shape=jax.ShapeDtypeStruct(shape, whole.dtype),
        scratch_shapes=[
            pltpu.VMEM((chips,) + block, whole.dtype),
            pltpu.SemaphoreType.DMA((chips,)),
            pltpu.SemaphoreType.DMA((chips,)),
        ],
        cost_estimate=BESIDE,
        compiler_params=pltpu.CompilerParams(vmem_limit_bytes=VMEM_LIMIT),
    )(plan, whole)


def query_kernel(bases, first, far, with_total, closing, plan_ref, *refs):
    sides = len(far)
    count = sum(len(group) for group in bases)
    blocks = refs[:count]
    weights = refs[count : count + sides]
    before = refs[count + sides : count + 2 * sides] if with_total else None
    if closing:
        keep, give, buf, sems, *totals = refs[-4 - sides :]
    else:
        totals, buf, sems = refs[-sides - 2 : -2], refs[-2], refs[-1]
    depth = buf.shape[1]
    core = plan_ref[plan_ref.shape[0] - 1]
    copies = []
    for i in range(len(bases)):
        for side in range(sides):
            block = plan_ref[first + i]
            block = block if far[side] else 2 * block + core
            rows = pl.ds(pl.multiple_of(block * depth, depth), depth)
            n = i * sides + side
            copies.append(pltpu.make_async_copy(weights[side].at[rows], buf.at[n], sems.at[n]))
    for copy in copies:
        copy.start()
    for side in range(sides):
        if with_total:
            totals[side][...] = before[side][...]
        else:
            totals[side][...] = jnp.zeros_like(totals[side])
    at = 0
    for i, group in enumerate(bases):
        for side in range(sides):
            n = i * sides + side
            copies[n].wait()
            for g, base in enumerate(group):
                rows = pl.ds(base, blocks[at + g].shape[0])
                totals[side][rows, :] += jnp.dot(
                    blocks[at + g][...], buf[n], preferred_element_type=f32
                )
        at += len(group)
    if not closing:
        return
    chips = (plan_ref.shape[0] - 1) // 2
    rows_here = totals[0].shape[0] // (2 * chips)
    heads = totals[0].shape[1] // HD

    def hand_out(side):
        for chip in range(chips):
            for to in range(2):
                target = keep if to == side else give
                rows = slice((2 * chip + to) * rows_here, (2 * chip + to + 1) * rows_here)
                for half in range(2):
                    source = totals[0 if half == side else 1]
                    for h in range(heads):
                        start = chip * rows_here * 2 * heads + half * heads + h
                        target[pl.ds(start, rows_here, 2 * heads), :] = source[
                            rows, h * HD : (h + 1) * HD
                        ]

    for side in range(2):
        pl.when(core == side)(functools.partial(hand_out, side))


def query_terms(totals, groups, w_own, w_far, plan, first, closing=False):
    blocks = [block for group in groups for block, _ in group]
    bases = [[base for _, base in group] for group in groups]
    depth = blocks[0].shape[1]
    rows = max(base + block.shape[0] for group in groups for block, base in group)
    weights = [w for w in (w_own, w_far) if w is not None]
    far = [w is w_far for w in weights]
    width = weights[0].shape[1]
    sides = len(weights)
    totals = list(totals) if totals is not None else []
    vmem = pl.BlockSpec(memory_space=pltpu.VMEM)
    shape = (rows * width // HD, HD) if closing else (rows, width)
    return pl.pallas_call(
        functools.partial(query_kernel, bases, first, far, bool(totals), closing),
        in_specs=[pl.BlockSpec(memory_space=pltpu.SMEM)]
        + [vmem] * len(blocks)
        + [pl.BlockSpec(memory_space=pl.ANY)] * sides
        + [vmem] * len(totals),
        out_specs=[vmem] * sides,
        out_shape=[jax.ShapeDtypeStruct(shape, f32)] * sides,
        scratch_shapes=[
            pltpu.VMEM((sides * len(groups), depth, width), bf16),
            pltpu.SemaphoreType.DMA((sides * len(groups),)),
        ]
        + [pltpu.VMEM((rows, width), f32)] * (sides if closing else 0),
        cost_estimate=BESIDE,
        compiler_params=pltpu.CompilerParams(vmem_limit_bytes=VMEM_LIMIT),
    )(plan, *blocks, *weights, *totals)


def out_kernel(first, amount, parts, opening, plan_ref, *refs):
    core = plan_ref[plan_ref.shape[0] - 1]
    if opening:
        mine, other, w_own, w_far = refs[:4]
        outs, lhs, (buf, sems, mixed, flat) = refs[4:-5], refs[-5], refs[-4:]
    else:
        lhs, w_own, w_far = refs[:3]
        outs, (buf, sems) = refs[3:-2], refs[-2:]
    width = buf.shape[3]
    copies = []
    for i in range(amount):
        block = plan_ref[first + i]
        for side, weights in enumerate((w_own, w_far)):
            column = block if side else 2 * block + core
            columns = pl.ds(pl.multiple_of(column * width, width), width)
            owner = 1 - core if side else core
            copies.append(
                pltpu.make_async_copy(weights.at[:, columns], buf.at[i, owner], sems.at[2 * i + side])
            )
    for copy in copies:
        copy.start()
    if opening:
        chips = (plan_ref.shape[0] - 1) // 2
        rows_here = lhs.shape[0] // (2 * chips)
        heads = lhs.shape[1] // HD
        halves = [mine[...].astype(f32), other[...].astype(f32)]
        for side in range(2):
            mixed[...] = jnp.where(core == side, halves[0], halves[1])
            for h in range(heads):
                columns = slice(h * HD, (h + 1) * HD)
                for chip in range(chips):
                    rows = slice((2 * chip + side) * rows_here, (2 * chip + side + 1) * rows_here)
                    start = chip * rows_here * heads + h
                    flat[rows, columns] = mixed[pl.ds(start, rows_here, heads), :]
        lhs[...] = flat[...].astype(bf16)
    for i in range(amount):
        copies[2 * i].wait()
        copies[2 * i + 1].wait()
        depth = buf.shape[2]
        value = jnp.dot(lhs[:, :depth], buf[i, 0], preferred_element_type=f32)
        value = value + jnp.dot(lhs[:, depth:], buf[i, 1], preferred_element_type=f32)
        rows = value.shape[0] // parts
        for p in range(parts):
            target = outs[i * parts + p]
            target[...] = value[p * rows : (p + 1) * rows].astype(target.dtype)


def out_terms(heads, w_own, w_far, plan, first, amount, width, kind, parts=1):
    opening = isinstance(heads, tuple)
    depth = w_own.shape[0]
    rows = 2 * heads[0].size // (2 * depth) if opening else heads.shape[0]
    vmem = pl.BlockSpec(memory_space=pltpu.VMEM)
    anywhere = pl.BlockSpec(memory_space=pl.ANY)
    args = list(heads) if opening else [heads]
    shapes = [jax.ShapeDtypeStruct((rows // parts, width), kind)] * (amount * parts)
    scratch = [
        pltpu.VMEM((amount, 2, depth, width), bf16),
        pltpu.SemaphoreType.DMA((2 * amount,)),
    ]
    if opening:
        shapes.append(jax.ShapeDtypeStruct((rows, 2 * depth), bf16))
        scratch += [pltpu.VMEM(heads[0].shape, f32), pltpu.VMEM((rows, 2 * depth), f32)]
    return pl.pallas_call(
        functools.partial(out_kernel, first, amount, parts, opening),
        in_specs=[pl.BlockSpec(memory_space=pltpu.SMEM)] + [vmem] * len(args) + [anywhere] * 2,
        out_specs=[vmem] * len(shapes),
        out_shape=shapes,
        scratch_shapes=scratch,
        cost_estimate=BESIDE,
        compiler_params=pltpu.CompilerParams(vmem_limit_bytes=VMEM_LIMIT),
    )(plan, *args, w_own, w_far)


def attend_kernel(
    source_ref, row_ref, length_ref,
    q_ref, cos_ref, sin_ref, new_ref, prefix_own, prefix_far, suffix_own, suffix_far,
    out_ref, prefix_buf, page_buf, q_buf, o_buf, prefix_sem, page_sem,
):
    prompts = prefix_buf.shape[0]
    chips = q_ref.shape[0]
    heads_here = HEADS // chips
    per_kv = chips // KV
    page = page_buf.shape[3]
    beam_rows = per_kv * heads_here

    def prefix_copies(j):
        return [
            pltpu.make_async_copy(prefix_own.at[0, j], prefix_buf.at[j, 0], prefix_sem.at[j, 0]),
            pltpu.make_async_copy(prefix_far.at[0, j], prefix_buf.at[j, 1], prefix_sem.at[j, 1]),
        ]

    def fetch(j):
        for copy in prefix_copies(j):
            copy.start()
        for b in range(HALF):
            r = j * HALF + b

            @pl.when(source_ref[r] == 0)
            def _():
                pltpu.make_async_copy(
                    suffix_own.at[row_ref[r]], page_buf.at[r], page_sem.at[r]
                ).start()

            @pl.when(source_ref[r] != 0)
            def _():
                pltpu.make_async_copy(
                    suffix_far.at[row_ref[r]], page_buf.at[r], page_sem.at[r]
                ).start()

    fetch(0)
    q_buf[...] = q_ref[...].astype(f32)
    position = lax.broadcasted_iota(jnp.int32, (beam_rows, page), 1)
    nt = (((1,), (1,)), ((), ()))

    for j in range(prompts):
        for copy in prefix_copies(j):
            copy.wait()
        for b in range(HALF):
            r = j * HALF + b
            pltpu.make_async_copy(suffix_own.at[0], page_buf.at[r], page_sem.at[r]).wait()
        if j + 1 < prompts:
            fetch(j + 1)

        def spread(ref, columns):
            return jnp.concatenate(
                [
                    jnp.broadcast_to(ref[r : r + 1, columns], (beam_rows, HD))
                    for r in range(j * HALF, (j + 1) * HALF)
                ],
                axis=0,
            )

        everything = slice(0, HD)
        cosine = spread(cos_ref, everything)
        sines = spread(sin_ref, everything)
        masks = [position < length_ref[j * HALF + b] for b in range(HALF)]
        for k in range(KV):
            spots = [
                (k * per_kv + t, slice((j * HALF + b) * heads_here, (j * HALF + b + 1) * heads_here))
                for b in range(HALF)
                for t in range(per_kv)
            ]
            query = jnp.concatenate([q_buf[chip, rows, :] for chip, rows in spots], axis=0)
            turned = query * cosine + pltpu.roll(query, HD // 2, 1) * sines
            turned = (turned * HD ** (-0.5)).astype(bf16)
            prefix_scores = [
                lax.dot_general(turned, prefix_buf[j, side, 0, k], nt, preferred_element_type=f32)
                for side in range(2)
            ]
            page_scores = jnp.concatenate(
                [
                    jnp.where(
                        masks[b],
                        lax.dot_general(
                            turned[b * beam_rows : (b + 1) * beam_rows],
                            page_buf[j * HALF + b, 0, k],
                            nt,
                            preferred_element_type=f32,
                        ),
                        big_negative,
                    )
                    for b in range(HALF)
                ],
                axis=0,
            )
            new_key = spread(new_ref, slice(k * HD, (k + 1) * HD))
            new_value = spread(new_ref, slice((KV + k) * HD, (KV + k + 1) * HD))
            new_score = jnp.sum(turned.astype(f32) * new_key, axis=1, keepdims=True)
            scores = prefix_scores + [page_scores]
            highest = new_score
            for score in scores:
                highest = jnp.maximum(highest, jnp.max(score, axis=1, keepdims=True))
            weights = [jnp.exp(score - highest) for score in scores]
            new_weight = jnp.exp(new_score - highest)
            weight_sum = new_weight
            for weight in weights:
                weight_sum = weight_sum + jnp.sum(weight, axis=1, keepdims=True)
            weighted = new_weight.astype(bf16).astype(f32) * new_value
            for side in range(2):
                weighted = weighted + jnp.dot(
                    weights[side].astype(bf16),
                    prefix_buf[j, side, 1, k],
                    preferred_element_type=f32,
                )
            page_weight = weights[2].astype(bf16)
            weighted = weighted + jnp.concatenate(
                [
                    jnp.dot(
                        page_weight[b * beam_rows : (b + 1) * beam_rows],
                        page_buf[j * HALF + b, 1, k],
                        preferred_element_type=f32,
                    )
                    for b in range(HALF)
                ],
                axis=0,
            )
            result = weighted / weight_sum
            for n, (chip, rows) in enumerate(spots):
                o_buf[chip, rows, :] = result[n * heads_here : (n + 1) * heads_here]
    out_ref[...] = o_buf[...].astype(bf16)


def attend(queries, cosine, sines, new_rows, prefix_own, prefix_far, suffix_own, suffix_far,
           source, row, page_len):
    rows = suffix_own.shape[0]
    prompts = rows // HALF
    part = prefix_own.shape[4]
    page = suffix_own.shape[3]
    vmem = pl.BlockSpec(memory_space=pltpu.VMEM)
    smem = pl.BlockSpec(memory_space=pltpu.SMEM)
    anywhere = pl.BlockSpec(memory_space=pl.ANY)
    keys = rows * (2 * part + page)
    return pl.pallas_call(
        attend_kernel,
        in_specs=[smem] * 3 + [vmem] * 4 + [anywhere] * 4,
        out_specs=vmem,
        out_shape=jax.ShapeDtypeStruct(queries.shape, bf16),
        scratch_shapes=[
            pltpu.VMEM((prompts, 2) + prefix_own.shape[2:], bf16),
            pltpu.VMEM(suffix_own.shape, bf16),
            pltpu.VMEM(queries.shape, f32),
            pltpu.VMEM(queries.shape, f32),
            pltpu.SemaphoreType.DMA((prompts, 2)),
            pltpu.SemaphoreType.DMA((rows,)),
        ],
        cost_estimate=pl.CostEstimate(
            flops=4 * keys * HEADS * HD,
            bytes_accessed=2 * prefix_own.size * 2 + 2 * suffix_own.size,
            transcendentals=keys * HEADS,
        ),
        compiler_params=pltpu.CompilerParams(vmem_limit_bytes=VMEM_LIMIT),
    )(source, row, page_len, queries, cosine, sines, new_rows,
      prefix_own, prefix_far, suffix_own, suffix_far)


def body(hidden, w_query, w_out, new_kv, prefix_kv, suffix_kv, parents, lengths):
    count = lax.axis_size("tensor")
    order = ring_chips(count // 2)
    chips = len(order)
    hops = chips // 2
    me = lax.axis_index("tensor")
    core = me % 2
    plan = lax.dynamic_index_in_dim(make_plan(order, hops), me, keepdims=False)

    onward, backward = along(order, 1), along(order, -1)
    to_core = [(t, t ^ 1) for t in range(count)]
    rows_all, depth = hidden.shape
    rows_here = new_kv.shape[0]
    prompts_here = rows_here // HALF
    prefix_len = 2 * prefix_kv.shape[4]

    def tables(far_len):
        own_len = lengths.reshape(prompts_here, HALF)
        far_len = far_len.reshape(prompts_here, HALF)
        parent = parents.reshape(prompts_here, HALF)
        slot = parent % HALF
        from_far = (parent // HALF) != core
        chosen = [
            jnp.sum(jnp.where(slot[..., None] == jnp.arange(HALF), table[:, None, :], 0), axis=-1)
            for table in (own_len, far_len)
        ]
        page_len = jnp.where(from_far, chosen[1], chosen[0]).reshape(rows_here)
        page_row = (jnp.arange(prompts_here, dtype=jnp.int32)[:, None] * HALF + slot).reshape(rows_here)
        source = from_far.astype(jnp.int32).reshape(rows_here)
        frequency = rope_base ** (-jnp.arange(HD // 2, dtype=f32) * 2.0 / HD)
        angles = (prefix_len + page_len).astype(f32)[:, None] * frequency
        cosine = jnp.cos(angles)
        sines = jnp.sin(angles)
        cosine = jnp.concatenate([cosine, cosine], axis=1)
        sines = jnp.concatenate([-sines, sines], axis=1)
        new_rows = new_kv.astype(f32).reshape(rows_here, 2 * KV * HD)
        return cosine, sines, new_rows, source, page_row, page_len

    cut = rows_all // 2
    a = b = hidden
    blocks = [[(hidden, 0)]]
    own_total = far_total = None
    own_done = far_done = 0
    for s in range(1, hops + 1):
        if s == hops:
            a, b = a[:cut], b[cut:]
        a, b = send(a, onward), send(b, backward)
        if s == 1:
            far_len = send(lengths, to_core)
            prefix_far = send(prefix_kv, to_core)
            wq_send = others_half(w_query, plan, chips, True)
            beside = tables(far_len)
            a, b, prefix_far, wq_send, *beside = tied(a, b, prefix_far, wq_send, *beside)
            cosine, sines, new_rows, source, page_row, page_len = beside
            wq_far = send(wq_send, to_core)
        else:
            beside = []
            fresh = blocks[own_done:]
            if s == 2:
                own_total = query_terms(None, fresh, w_query, None, plan, 0)
                w_whole, *own_total = tied(w_out, *own_total)
                wo_send = others_half(w_whole, plan, chips, False)
                beside = [wo_send]
            elif s == 3:
                own_total = query_terms(own_total, fresh, w_query, None, plan, own_done)
                far_total = list(query_terms(None, blocks, None, wq_far, plan, 0))
            else:
                own_total, far_total = query_terms(
                    own_total + far_total, fresh, w_query, wq_far, plan, own_done
                )
                own_total, far_total = [own_total], [far_total]
            far_total = far_total or []
            a, b, *beside = tied(a, b, *own_total, *far_total, *beside)
            own_total, beside = beside[:1], beside[1:]
            if s > 2:
                far_total, beside = beside[:1], beside[1:]
            if s == 2:
                wo_send, suffix_in = tied(*beside, suffix_kv)
                wo_far = send(wo_send, to_core)
                suffix_far = send(suffix_in, to_core)
            own_done = len(blocks)
        if s < hops:
            blocks += [[(a, 0)], [(b, 0)]]
        else:
            blocks.append([(a, 0), (b, cut)])
    keep, give = query_terms(
        own_total + far_total, blocks[own_done:], w_query, wq_far, plan, own_done, True
    )
    query = (keep + send(give, to_core)).astype(bf16).reshape(chips, -1, HD)
    same_core = [[2 * chip + side for chip in range(chips)] for side in range(2)]

    def exchange(values):
        return lax.all_to_all(
            values, "tensor", split_axis=0, concat_axis=0, axis_index_groups=same_core, tiled=True
        )

    query, suffix_far, wo_far = tied(query, suffix_far, wo_far)
    heads = exchange(
        attend(exchange(query), cosine, sines, new_rows, prefix_kv, prefix_far, suffix_kv,
               suffix_far, source, page_row, page_len)
    ).reshape(-1, HD)
    heads = (heads, send(heads, to_core))

    width = w_out.shape[1] // count

    def out(heads, first, amount, kind, parts=1):
        return out_terms(heads, w_out, wo_far, plan, chips + first, amount, width, kind, parts)

    up, down, heads = tied(*out(heads, 0, 1, bf16, 2))
    a, b = send(up, onward), send(down, backward)
    for s in range(hops - 1, 0, -1):
        up, down = out(heads, 1 + 2 * (hops - 1 - s), 2, f32)
        a, b, up, down = tied(a, b, up, down)
        a, b = a.astype(f32), b.astype(f32)
        if s == hops - 1:
            up = jnp.concatenate([up[:cut] + a, up[cut:]], axis=0)
            down = jnp.concatenate([down[:cut], down[cut:] + b], axis=0)
        else:
            up, down = up + a, down + b
        a, b = tied(up.astype(bf16), down.astype(bf16))
        a, b = send(a, onward), send(b, backward)
    [own_term] = out(heads, chips - 1, 1, f32)
    a, b, own_term = tied(a, b, own_term)
    return (own_term + a.astype(f32) + b.astype(f32)).astype(bf16)


def solution(mesh):
    return jax.shard_map(
        body,
        mesh=mesh,
        in_specs=(
            P("groups", "tensor"),
            P(None, "tensor"),
            P("tensor", None),
            P(("groups", "tensor"), None, None, None),
            P(("groups", "tensor"), None, None, None, None, None),
            P(("groups", "tensor"), None, None, None, None),
            P(("groups", "tensor")),
            P(("groups", "tensor")),
        ),
        out_specs=P("groups", "tensor"),
        check_vma=False,
    )
```

```python
import functools

import jax
import jax.numpy as jnp
from jax import lax
from jax.experimental import pallas as pl
from jax.experimental.pallas import tpu as pltpu
from jax.sharding import PartitionSpec as P

HEADS = 64
KV = 4
HD = 128
BEAMS = 8
HALF = BEAMS // 2

rope_base = 500000.0
big_negative = -1e30
f32 = jnp.float32
bf16 = jnp.bfloat16
MIB = 1024 * 1024
VMEM_LIMIT = 48 * MIB
BESIDE = pl.CostEstimate(flops=1000, bytes_accessed=1000, transcendentals=0)


def ring_chips(count):
    if count == 8:
        return [0, 2, 4, 6, 7, 5, 3, 1]
    return list(range(count))


def send(block, route):
    return lax.ppermute(block, "tensor", route)


def tied(*values):
    return lax.optimization_barrier(values)


def along(order, step):
    count = len(order)
    return [
        (2 * order[i] + c, 2 * order[(i + step) % count] + c)
        for i in range(count)
        for c in range(2)
    ]


def make_plan(order, hops):
    chips = len(order)
    arrive = [0] + [d for s in range(1, hops) for d in (-s, s)] + [hops]
    leave = [hops] + [d for s in range(hops - 1, 0, -1) for d in (s, -s)] + [0]
    rows = []
    for t in range(2 * chips):
        at = order.index(t // 2)
        rows.append([order[(at + d) % chips] for d in arrive + leave] + [t % 2])
    return jnp.asarray(rows, jnp.int32)


def split_kernel(chips, by_rows, plan_ref, whole, part, buf, in_sems, out_sems):
    other = 1 - plan_ref[2 * chips]
    size = (part.shape[0] if by_rows else part.shape[1]) // chips
    ins, outs = [], []
    for i in range(chips):
        start = pl.multiple_of((2 * i + other) * size, size)
        if by_rows:
            source, target = whole.at[pl.ds(start, size)], part.at[pl.ds(i * size, size)]
        else:
            source, target = whole.at[:, pl.ds(start, size)], part.at[:, pl.ds(i * size, size)]
        ins.append(pltpu.make_async_copy(source, buf.at[i], in_sems.at[i]))
        outs.append(pltpu.make_async_copy(buf.at[i], target, out_sems.at[i]))
    for copy in ins:
        copy.start()
    for before, after in zip(ins, outs):
        before.wait()
        after.start()
    for copy in outs:
        copy.wait()


def others_half(whole, plan, chips, by_rows):
    shape = (whole.shape[0] // 2, whole.shape[1]) if by_rows else (whole.shape[0], whole.shape[1] // 2)
    block = (shape[0] // chips, shape[1]) if by_rows else (shape[0], shape[1] // chips)
    anywhere = pl.BlockSpec(memory_space=pl.ANY)
    return pl.pallas_call(
        functools.partial(split_kernel, chips, by_rows),
        in_specs=[pl.BlockSpec(memory_space=pltpu.SMEM), anywhere],
        out_specs=anywhere,
        out_shape=jax.ShapeDtypeStruct(shape, whole.dtype),
        scratch_shapes=[
            pltpu.VMEM((chips,) + block, whole.dtype),
            pltpu.SemaphoreType.DMA((chips,)),
            pltpu.SemaphoreType.DMA((chips,)),
        ],
        cost_estimate=BESIDE,
        compiler_params=pltpu.CompilerParams(vmem_limit_bytes=VMEM_LIMIT),
    )(plan, whole)


def query_kernel(bases, first, far, with_total, fetching, closing, plan_ref, *refs):
    sides = len(far)
    if fetching:
        *refs, next_sems = refs
        *refs, next_weights, buf, sems = refs
        refs = refs + [buf, sems]
    count = sum(len(group) for group in bases)
    blocks = refs[:count]
    operands = 1 if closing else sides
    weights = refs[count : count + operands]
    before = refs[count + operands : count + operands + sides] if with_total else None
    if closing:
        keep, give, *totals = refs[-2 - sides :]
        buf = weights[0]
    else:
        totals, buf, sems = refs[-sides - 2 : -2], refs[-2], refs[-1]
    depth = buf.shape[1]
    core = plan_ref[plan_ref.shape[0] - 1]
    copies = []
    for i in range(0 if closing else len(bases)):
        for side in range(sides):
            block = plan_ref[first + i]
            block = block if far[side] else 2 * block + core
            rows = pl.ds(pl.multiple_of(block * depth, depth), depth)
            n = i * sides + side
            copies.append(pltpu.make_async_copy(weights[side].at[rows], buf.at[n], sems.at[n]))
    later = []
    if fetching:
        for side in range(sides):
            block = plan_ref[first + len(bases)]
            block = block if far[side] else 2 * block + core
            rows = pl.ds(pl.multiple_of(block * depth, depth), depth)
            later.append(
                pltpu.make_async_copy(
                    weights[side].at[rows], next_weights.at[side], next_sems.at[side]
                )
            )
    for copy in copies + later:
        copy.start()
    for side in range(sides):
        if with_total:
            totals[side][...] = before[side][...]
        else:
            totals[side][...] = jnp.zeros_like(totals[side])
    at = 0
    for i, group in enumerate(bases):
        for side in range(sides):
            n = i * sides + side
            if not closing:
                copies[n].wait()
            for g, base in enumerate(group):
                rows = pl.ds(base, blocks[at + g].shape[0])
                totals[side][rows, :] += jnp.dot(
                    blocks[at + g][...], buf[n], preferred_element_type=f32
                )
        at += len(group)
    for copy in later:
        copy.wait()
    if not closing:
        return
    chips = (plan_ref.shape[0] - 1) // 2
    rows_here = totals[0].shape[0] // (2 * chips)
    heads = totals[0].shape[1] // HD

    def hand_out(side):
        for chip in range(chips):
            for to in range(2):
                target = keep if to == side else give
                rows = slice((2 * chip + to) * rows_here, (2 * chip + to + 1) * rows_here)
                for half in range(2):
                    source = totals[0 if half == side else 1]
                    for h in range(heads):
                        start = chip * rows_here * 2 * heads + half * heads + h
                        target[pl.ds(start, rows_here, 2 * heads), :] = source[
                            rows, h * HD : (h + 1) * HD
                        ]

    for side in range(2):
        pl.when(core == side)(functools.partial(hand_out, side))


def query_terms(totals, groups, w_own, w_far, plan, first, fetched=None, fetching=False):
    closing = fetched is not None
    blocks = [block for group in groups for block, _ in group]
    bases = [[base for _, base in group] for group in groups]
    depth = blocks[0].shape[1]
    rows = max(base + block.shape[0] for group in groups for block, base in group)
    weights = [w for w in (w_own, w_far) if w is not None]
    far = [w is w_far for w in weights]
    width = weights[0].shape[1]
    sides = len(weights)
    totals = list(totals) if totals is not None else []
    vmem = pl.BlockSpec(memory_space=pltpu.VMEM)
    shape = (rows * width // HD, HD) if closing else (rows, width)
    if closing:
        weights = [fetched]
        scratch = [pltpu.VMEM((rows, width), f32)] * sides
    else:
        scratch = [
            pltpu.VMEM((sides * len(groups), depth, width), bf16),
            pltpu.SemaphoreType.DMA((sides * len(groups),)),
        ] + [pltpu.SemaphoreType.DMA((sides,))] * fetching
    return pl.pallas_call(
        functools.partial(query_kernel, bases, first, far, bool(totals), fetching, closing),
        in_specs=[pl.BlockSpec(memory_space=pltpu.SMEM)]
        + [vmem] * len(blocks)
        + ([vmem] if closing else [pl.BlockSpec(memory_space=pl.ANY)] * sides)
        + [vmem] * len(totals),
        out_specs=[vmem] * (sides + fetching),
        out_shape=[jax.ShapeDtypeStruct(shape, f32)] * sides
        + [jax.ShapeDtypeStruct((sides, depth, width), bf16)] * fetching,
        scratch_shapes=scratch,
        cost_estimate=BESIDE,
        compiler_params=pltpu.CompilerParams(vmem_limit_bytes=VMEM_LIMIT),
    )(plan, *blocks, *weights, *totals)


def column_copies(plan_ref, position, width, w_own, w_far, target, sems):
    core = plan_ref[plan_ref.shape[0] - 1]
    chip = plan_ref[position]
    copies = []
    for side, (weights, column, owner) in enumerate(
        ((w_own, 2 * chip + core, core), (w_far, chip, 1 - core))
    ):
        columns = pl.ds(pl.multiple_of(column * width, width), width)
        copies.append(
            pltpu.make_async_copy(weights.at[:, columns], target.at[owner], sems.at[side])
        )
    return copies


def column_kernel(first, plan_ref, w_own, w_far, target, sems):
    copies = column_copies(plan_ref, first, target.shape[2], w_own, w_far, target, sems)
    for copy in copies:
        copy.start()
    for copy in copies:
        copy.wait()


def first_columns(w_own, w_far, plan, first, width):
    anywhere = pl.BlockSpec(memory_space=pl.ANY)
    return pl.pallas_call(
        functools.partial(column_kernel, first),
        in_specs=[pl.BlockSpec(memory_space=pltpu.SMEM)] + [anywhere] * 2,
        out_specs=pl.BlockSpec(memory_space=pltpu.VMEM),
        out_shape=jax.ShapeDtypeStruct((2, w_own.shape[0], width), bf16),
        scratch_shapes=[pltpu.SemaphoreType.DMA((2,))],
        cost_estimate=BESIDE,
        compiler_params=pltpu.CompilerParams(vmem_limit_bytes=VMEM_LIMIT),
    )(plan, w_own, w_far)


def opening_kernel(parts, plan_ref, mine, other, columns_ref, *refs):
    outs, lhs, mixed, flat = refs[:-3], refs[-3], refs[-2], refs[-1]
    core = plan_ref[plan_ref.shape[0] - 1]
    chips = (plan_ref.shape[0] - 1) // 2
    rows_here = lhs.shape[0] // (2 * chips)
    heads = lhs.shape[1] // HD
    halves = [mine[...].astype(f32), other[...].astype(f32)]
    for side in range(2):
        mixed[side] = jnp.where(core == side, halves[0], halves[1])
        for h in range(heads):
            for chip in range(chips):
                rows = slice((2 * chip + side) * rows_here, (2 * chip + side + 1) * rows_here)
                start = chip * rows_here * heads + h
                flat[rows, h * HD : (h + 1) * HD] = mixed[side, pl.ds(start, rows_here, heads), :]
    lhs[...] = flat[...].astype(bf16)
    depth = columns_ref.shape[1]
    value = jnp.dot(lhs[:, :depth], columns_ref[0], preferred_element_type=f32)
    value = value + jnp.dot(lhs[:, depth:], columns_ref[1], preferred_element_type=f32)
    rows = value.shape[0] // parts
    for p in range(parts):
        outs[p][...] = value[p * rows : (p + 1) * rows].astype(bf16)


def opening_terms(mine, other, columns, plan, parts):
    depth, width = columns.shape[1:]
    rows = mine.size // depth
    vmem = pl.BlockSpec(memory_space=pltpu.VMEM)
    return pl.pallas_call(
        functools.partial(opening_kernel, parts),
        in_specs=[pl.BlockSpec(memory_space=pltpu.SMEM)] + [vmem] * 3,
        out_specs=[vmem] * (parts + 1),
        out_shape=[jax.ShapeDtypeStruct((rows // parts, width), bf16)] * parts
        + [jax.ShapeDtypeStruct((rows, 2 * depth), bf16)],
        scratch_shapes=[
            pltpu.VMEM((2,) + mine.shape, f32),
            pltpu.VMEM((rows, 2 * depth), f32),
        ],
        cost_estimate=BESIDE,
        compiler_params=pltpu.CompilerParams(vmem_limit_bytes=VMEM_LIMIT),
    )(plan, mine, other, columns)


def out_kernel(first, amount, plan_ref, lhs, w_own, w_far, *refs):
    outs, buf, sems = refs[:-2], refs[-2], refs[-1]
    depth, width = buf.shape[2:]
    copies = [
        column_copies(plan_ref, first + i, width, w_own, w_far, buf.at[i], sems.at[i])
        for i in range(amount)
    ]
    for pair in copies:
        for copy in pair:
            copy.start()
    for i in range(amount):
        for copy in copies[i]:
            copy.wait()
        value = jnp.dot(lhs[:, :depth], buf[i, 0], preferred_element_type=f32)
        outs[i][...] = value + jnp.dot(lhs[:, depth:], buf[i, 1], preferred_element_type=f32)


def out_terms(heads, w_own, w_far, plan, first, amount, width):
    depth = w_own.shape[0]
    rows = heads.shape[0]
    vmem = pl.BlockSpec(memory_space=pltpu.VMEM)
    anywhere = pl.BlockSpec(memory_space=pl.ANY)
    return pl.pallas_call(
        functools.partial(out_kernel, first, amount),
        in_specs=[pl.BlockSpec(memory_space=pltpu.SMEM), vmem] + [anywhere] * 2,
        out_specs=[vmem] * amount,
        out_shape=[jax.ShapeDtypeStruct((rows, width), f32)] * amount,
        scratch_shapes=[
            pltpu.VMEM((amount, 2, depth, width), bf16),
            pltpu.SemaphoreType.DMA((amount, 2)),
        ],
        cost_estimate=BESIDE,
        compiler_params=pltpu.CompilerParams(vmem_limit_bytes=VMEM_LIMIT),
    )(plan, heads, w_own, w_far)


def attend_kernel(
    source_ref, row_ref, length_ref,
    q_ref, cos_ref, sin_ref, new_ref, prefix_own, prefix_far, suffix_own, suffix_far,
    out_ref, prefix_buf, page_buf, q_buf, o_buf, prefix_sem, page_sem,
):
    prompts = prefix_buf.shape[0]
    chips = q_ref.shape[0]
    heads_here = HEADS // chips
    per_kv = chips // KV
    page = page_buf.shape[3]
    beam_rows = per_kv * heads_here

    def prefix_copies(j):
        return [
            pltpu.make_async_copy(prefix_own.at[0, j], prefix_buf.at[j, 0], prefix_sem.at[j, 0]),
            pltpu.make_async_copy(prefix_far.at[0, j], prefix_buf.at[j, 1], prefix_sem.at[j, 1]),
        ]

    def fetch(j):
        for copy in prefix_copies(j):
            copy.start()
        for b in range(HALF):
            r = j * HALF + b

            @pl.when(source_ref[r] == 0)
            def _():
                pltpu.make_async_copy(
                    suffix_own.at[row_ref[r]], page_buf.at[r], page_sem.at[r]
                ).start()

            @pl.when(source_ref[r] != 0)
            def _():
                pltpu.make_async_copy(
                    suffix_far.at[row_ref[r]], page_buf.at[r], page_sem.at[r]
                ).start()

    for j in range(prompts):
        fetch(j)
    q_buf[...] = q_ref[...].astype(f32)
    position = lax.broadcasted_iota(jnp.int32, (beam_rows, page), 1)
    nt = (((1,), (1,)), ((), ()))

    for j in range(prompts):
        for copy in prefix_copies(j):
            copy.wait()
        for b in range(HALF):
            r = j * HALF + b
            pltpu.make_async_copy(suffix_own.at[0], page_buf.at[r], page_sem.at[r]).wait()

        def spread(ref, columns):
            return jnp.concatenate(
                [
                    jnp.broadcast_to(ref[r : r + 1, columns], (beam_rows, HD))
                    for r in range(j * HALF, (j + 1) * HALF)
                ],
                axis=0,
            )

        everything = slice(0, HD)
        cosine = spread(cos_ref, everything)
        sines = spread(sin_ref, everything)
        masks = [position < length_ref[j * HALF + b] for b in range(HALF)]
        def place(k):
            return [
                (k * per_kv + t, slice((j * HALF + b) * heads_here, (j * HALF + b + 1) * heads_here))
                for b in range(HALF)
                for t in range(per_kv)
            ]

        def score(k):
            query = jnp.concatenate([q_buf[chip, rows, :] for chip, rows in place(k)], axis=0)
            turned = query * cosine + pltpu.roll(query, HD // 2, 1) * sines
            turned = (turned * HD ** (-0.5)).astype(bf16)
            prefix_scores = [
                lax.dot_general(turned, prefix_buf[j, side, 0, k], nt, preferred_element_type=f32)
                for side in range(2)
            ]
            page_scores = jnp.concatenate(
                [
                    jnp.where(
                        masks[b],
                        lax.dot_general(
                            turned[b * beam_rows : (b + 1) * beam_rows],
                            page_buf[j * HALF + b, 0, k],
                            nt,
                            preferred_element_type=f32,
                        ),
                        big_negative,
                    )
                    for b in range(HALF)
                ],
                axis=0,
            )
            new_key = spread(new_ref, slice(k * HD, (k + 1) * HD))
            new_score = jnp.sum(turned.astype(f32) * new_key, axis=1, keepdims=True)
            return prefix_scores + [page_scores], new_score

        def weigh(scores, new_score):
            highest = new_score
            for each in scores:
                highest = jnp.maximum(highest, jnp.max(each, axis=1, keepdims=True))
            weights = [jnp.exp(each - highest) for each in scores]
            new_weight = jnp.exp(new_score - highest)
            weight_sum = new_weight
            for weight in weights:
                weight_sum = weight_sum + jnp.sum(weight, axis=1, keepdims=True)
            return [weight.astype(bf16) for weight in weights], new_weight, weight_sum

        def gather(k, weights, new_weight, weight_sum):
            new_value = spread(new_ref, slice((KV + k) * HD, (KV + k + 1) * HD))
            weighted = new_weight.astype(bf16).astype(f32) * new_value
            for side in range(2):
                weighted = weighted + jnp.dot(
                    weights[side], prefix_buf[j, side, 1, k], preferred_element_type=f32
                )
            weighted = weighted + jnp.concatenate(
                [
                    jnp.dot(
                        weights[2][b * beam_rows : (b + 1) * beam_rows],
                        page_buf[j * HALF + b, 1, k],
                        preferred_element_type=f32,
                    )
                    for b in range(HALF)
                ],
                axis=0,
            )
            result = weighted / weight_sum
            for n, (chip, rows) in enumerate(place(k)):
                o_buf[chip, rows, :] = result[n * heads_here : (n + 1) * heads_here]

        ahead = score(0)
        for k in range(KV):
            now = ahead
            if k + 1 < KV:
                ahead = score(k + 1)
            gather(k, *weigh(*now))
    out_ref[...] = o_buf[...].astype(bf16)


def attend(queries, cosine, sines, new_rows, prefix_own, prefix_far, suffix_own, suffix_far,
           source, row, page_len):
    rows = suffix_own.shape[0]
    prompts = rows // HALF
    part = prefix_own.shape[4]
    page = suffix_own.shape[3]
    vmem = pl.BlockSpec(memory_space=pltpu.VMEM)
    smem = pl.BlockSpec(memory_space=pltpu.SMEM)
    anywhere = pl.BlockSpec(memory_space=pl.ANY)
    keys = rows * (2 * part + page)
    return pl.pallas_call(
        attend_kernel,
        in_specs=[smem] * 3 + [vmem] * 4 + [anywhere] * 4,
        out_specs=vmem,
        out_shape=jax.ShapeDtypeStruct(queries.shape, bf16),
        scratch_shapes=[
            pltpu.VMEM((prompts, 2) + prefix_own.shape[2:], bf16),
            pltpu.VMEM(suffix_own.shape, bf16),
            pltpu.VMEM(queries.shape, f32),
            pltpu.VMEM(queries.shape, f32),
            pltpu.SemaphoreType.DMA((prompts, 2)),
            pltpu.SemaphoreType.DMA((rows,)),
        ],
        cost_estimate=pl.CostEstimate(
            flops=4 * keys * HEADS * HD,
            bytes_accessed=2 * prefix_own.size * 2 + 2 * suffix_own.size,
            transcendentals=keys * HEADS,
        ),
        compiler_params=pltpu.CompilerParams(vmem_limit_bytes=VMEM_LIMIT),
    )(source, row, page_len, queries, cosine, sines, new_rows,
      prefix_own, prefix_far, suffix_own, suffix_far)


def body(hidden, w_query, w_out, new_kv, prefix_kv, suffix_kv, parents, lengths):
    count = lax.axis_size("tensor")
    order = ring_chips(count // 2)
    chips = len(order)
    hops = chips // 2
    me = lax.axis_index("tensor")
    core = me % 2
    plan = lax.dynamic_index_in_dim(make_plan(order, hops), me, keepdims=False)

    onward, backward = along(order, 1), along(order, -1)
    to_core = [(t, t ^ 1) for t in range(count)]
    rows_all, depth = hidden.shape
    rows_here = new_kv.shape[0]
    prompts_here = rows_here // HALF
    prefix_len = 2 * prefix_kv.shape[4]

    def tables(far_len):
        own_len = lengths.reshape(prompts_here, HALF)
        far_len = far_len.reshape(prompts_here, HALF)
        parent = parents.reshape(prompts_here, HALF)
        slot = parent % HALF
        from_far = (parent // HALF) != core
        chosen = [
            jnp.sum(jnp.where(slot[..., None] == jnp.arange(HALF), table[:, None, :], 0), axis=-1)
            for table in (own_len, far_len)
        ]
        page_len = jnp.where(from_far, chosen[1], chosen[0]).reshape(rows_here)
        page_row = (jnp.arange(prompts_here, dtype=jnp.int32)[:, None] * HALF + slot).reshape(rows_here)
        source = from_far.astype(jnp.int32).reshape(rows_here)
        frequency = rope_base ** (-jnp.arange(HD // 2, dtype=f32) * 2.0 / HD)
        angles = (prefix_len + page_len).astype(f32)[:, None] * frequency
        cosine = jnp.cos(angles)
        sines = jnp.sin(angles)
        cosine = jnp.concatenate([cosine, cosine], axis=1)
        sines = jnp.concatenate([-sines, sines], axis=1)
        new_rows = new_kv.astype(f32).reshape(rows_here, 2 * KV * HD)
        return cosine, sines, new_rows, source, page_row, page_len

    cut = rows_all // 2
    a = b = hidden
    blocks = [[(hidden, 0)]]
    own_total = far_total = None
    own_done = far_done = 0
    for s in range(1, hops + 1):
        if s == hops:
            a, b = a[:cut], b[cut:]
        a, b = send(a, onward), send(b, backward)
        if s == 1:
            far_len = send(lengths, to_core)
            prefix_far = send(prefix_kv, to_core)
            wq_send = others_half(w_query, plan, chips, True)
            beside = tables(far_len)
            a, b, prefix_far, wq_send, *beside = tied(a, b, prefix_far, wq_send, *beside)
            cosine, sines, new_rows, source, page_row, page_len = beside
            wq_far = send(wq_send, to_core)
        else:
            beside = []
            fresh = blocks[own_done:]
            if s == 2:
                own_total = query_terms(None, fresh, w_query, None, plan, 0)
                w_whole, *own_total = tied(w_out, *own_total)
                wo_send = others_half(w_whole, plan, chips, False)
                beside = [wo_send]
            elif s == 3:
                own_total = query_terms(own_total, fresh, w_query, None, plan, own_done)
                far_total = list(query_terms(None, blocks, None, wq_far, plan, 0))
            else:
                own_total, far_total, *fetched = query_terms(
                    own_total + far_total, fresh, w_query, wq_far, plan, own_done, None, s == hops
                )
                own_total, far_total = [own_total], [far_total]
            far_total = far_total or []
            a, b, *beside = tied(a, b, *own_total, *far_total, *beside)
            own_total, beside = beside[:1], beside[1:]
            if s > 2:
                far_total, beside = beside[:1], beside[1:]
            if s == 2:
                wo_send, suffix_in = tied(*beside, suffix_kv)
                suffix_far = send(suffix_in, to_core)
            own_done = len(blocks)
        if s < hops:
            blocks += [[(a, 0)], [(b, 0)]]
        else:
            blocks.append([(a, 0), (b, cut)])
    keep, give = query_terms(
        own_total + far_total, blocks[own_done:], w_query, wq_far, plan, own_done, *fetched
    )
    query = (keep + send(give, to_core)).astype(bf16).reshape(chips, -1, HD)
    same_core = [[2 * chip + side for chip in range(chips)] for side in range(2)]

    def exchange(values):
        return lax.all_to_all(
            values, "tensor", split_axis=0, concat_axis=0, axis_index_groups=same_core, tiled=True
        )

    query, suffix_far, wo_send = tied(query, suffix_far, wo_send)
    wo_far = send(wo_send, to_core)
    heads = exchange(
        attend(exchange(query), cosine, sines, new_rows, prefix_kv, prefix_far, suffix_kv,
               suffix_far, source, page_row, page_len)
    ).reshape(-1, HD)
    width = w_out.shape[1] // count
    heads, w_whole = tied(heads, w_out)
    columns = first_columns(w_whole, wo_far, plan, chips, width)
    other, columns = tied(send(heads, to_core), columns)

    def out(first, amount):
        return out_terms(heads, w_out, wo_far, plan, chips + first, amount, width)

    up, down, heads = tied(*opening_terms(heads, other, columns, plan, 2))
    a, b = send(up, onward), send(down, backward)
    for s in range(hops - 1, 0, -1):
        up, down = out(1 + 2 * (hops - 1 - s), 2)
        a, b, up, down = tied(a, b, up, down)
        a, b = a.astype(f32), b.astype(f32)
        if s == hops - 1:
            up = jnp.concatenate([up[:cut] + a, up[cut:]], axis=0)
            down = jnp.concatenate([down[:cut], down[cut:] + b], axis=0)
        else:
            up, down = up + a, down + b
        a, b = tied(up.astype(bf16), down.astype(bf16))
        a, b = send(a, onward), send(b, backward)
    [own_term] = out(chips - 1, 1)
    a, b, own_term = tied(a, b, own_term)
    return (own_term + a.astype(f32) + b.astype(f32)).astype(bf16)


def solution(mesh):
    return jax.shard_map(
        body,
        mesh=mesh,
        in_specs=(
            P("groups", "tensor"),
            P(None, "tensor"),
            P("tensor", None),
            P(("groups", "tensor"), None, None, None),
            P(("groups", "tensor"), None, None, None, None, None),
            P(("groups", "tensor"), None, None, None, None),
            P(("groups", "tensor")),
            P(("groups", "tensor")),
        ),
        out_specs=P("groups", "tensor"),
        check_vma=False,
    )
```
